32 devices in a mesh: gx: 8 (over z, core), gy: 4 (over y, x).
Axes of the slice: x: 2, y: 2, z: 4, core: 2. Of those that a mesh axis runs over, the one named last changes fastest.
Arguments:
- demand: float32 [16, 1024, 16384], P(None, 'gx', 'gy'), may hold values from -200 to 200, as said below
- initial: float32 [1024, 256], replicated, may hold values from -6 to 6
Outputs:
- factor: float32 [1024, 256], replicated
- core: float32 [256, 16, 16384], P('gx', None, 'gy')
The draws below stay inside these ranges and needn't reach their ends.
Inputs may be any that keep to these rules, and one draw needn't show every extreme that they name: `demand`: Real-valued fluctuations of order one to a few, not all of one scale along x.
All inputs are finite; a program needn't handle non-finite values.
Results may differ from the reference program's by a relative error of at most 0.0003.
Values sent between devices are 32-bit elements; how exact they have to be, the bound alone decides.
A program may use at most 128 MiB of HBM per device.

```python
import math
import jax
import jax.numpy as jnp
from jax import lax

NX = 1024
NY = 1024
L = 16
R = 256
S = 16
ITERS = 3


def draw_demand(key, part):
    keys = jax.random.split(key, 4)
    noise = jnp.clip(jax.random.normal(keys[0], (L, NX, S * NY), jnp.float32), -6.0, 6.0)
    upper = math.log(3.0)
    scales = jnp.exp(jax.random.uniform(keys[1], (1, NX, 1), jnp.float32, 0.0, upper))
    coefs = 0.7 * jnp.clip(jax.random.normal(keys[2], (4, 1, NX, 1), jnp.float32), -3.0, 3.0)
    factors = jnp.clip(jax.random.normal(keys[3], (4, L, 1, S * NY), jnp.float32), -4.0, 4.0)
    shared = noise
    for index_value in range(4):
        shared = shared + coefs[index_value] * factors[index_value]
    return (scales * shared).astype(jnp.float32)


def centred(stream_key, dims, deviation, reach, dtype=jnp.bfloat16):
    return jnp.clip(deviation * jax.random.normal(stream_key, dims, jnp.float32), -reach, reach).astype(dtype)


def setup_inputs(seed: int = 0) -> dict:
    seeds = jax.random.split(jax.random.key(seed), 3)
    demand = draw_demand(jax.random.fold_in(seeds[2], 71), 0)
    initial = centred(seeds[1], (NX, R), 1.0, 6.0, jnp.float32)
    return {"demand": demand, "initial": initial}


def orthonormal(block):
    weights = jnp.dot(block.T.astype(jnp.float32), block.astype(jnp.float32), precision=lax.Precision.HIGHEST, preferred_element_type=jnp.float32)
    lower_factor = jnp.linalg.cholesky(weights)
    return lax.linalg.triangular_solve(lower_factor, block, left_side=False, lower=True, transpose_a=True)

def reference(demand, initial):

    def add_layer(total, layer):
        return (total + jnp.einsum('xc,zc->xz', layer.astype(jnp.float32), layer.astype(jnp.float32), precision=lax.Precision.HIGHEST, preferred_element_type=jnp.float32), None)
    gram, unused = lax.scan(add_layer, jnp.zeros((NX, NX), jnp.float32), demand)
    gram = gram * (1.0 / (L * S * NY))
    basis = initial
    for iteration in range(ITERS):
        basis = orthonormal(jnp.dot(gram.astype(jnp.float32), basis.astype(jnp.float32), precision=lax.Precision.HIGHEST, preferred_element_type=jnp.float32))

    def project(layer):
        return jnp.einsum('xr,xc->rc', basis.astype(jnp.float32), layer.astype(jnp.float32), precision=lax.Precision.HIGHEST, preferred_element_type=jnp.float32)
    projected = lax.map(project, demand)
    return (basis, jnp.transpose(projected, (1, 0, 2)))
```

```python
import functools

import jax
import jax.numpy as jnp
from jax import lax
from jax.experimental import pallas as pl
from jax.experimental.pallas import tpu as pltpu
from jax.sharding import PartitionSpec as P

ITERS = 3
TILE = 256
PANEL = 32
WINDOW = 3
MESH = pl.DeviceIdType.MESH
HIGHEST = lax.Precision.HIGHEST


def dot(left, right, dims):
    return lax.dot_general(
        left, right, (dims, ((), ())), precision=HIGHEST, preferred_element_type=jnp.float32
    )


def chunk_columns(layers, columns):
    return min(columns, max(128, layers * columns // 8))


def far_first(n):
    return sorted(range(1, n), key=lambda p: (abs(p - n // 2), p))


def enter(n, me):
    barrier = pltpu.get_barrier_semaphore()
    for p in range(1, n):
        pl.semaphore_signal(
            barrier, inc=1, device_id={"gx": lax.rem(me + p, n)}, device_id_type=MESH
        )
    pl.semaphore_wait(barrier, n - 1)


def exchange_gram_kernel(
    n, layers, width, scale, demand, regrouped, gram, block, send_sems, recv_sems, self_sem, load_sem
):
    me = lax.axis_index("gx")
    rows, columns = demand.shape[1], demand.shape[2]
    per_layer = columns // width
    chunks = layers * per_layer
    order = far_first(n)

    def place(c):
        return lax.div(c, per_layer), pl.multiple_of(lax.rem(c, per_layer) * width, width)

    def outgoing(c, p):
        layer, column = place(c)
        target = lax.rem(me + p, n)
        return pltpu.make_async_remote_copy(
            src_ref=demand.at[target * layers + layer, :, pl.ds(column, width)],
            dst_ref=regrouped.at[layer, pl.ds(pl.multiple_of(me * rows, rows), rows), pl.ds(column, width)],
            send_sem=send_sems.at[c, p - 1],
            recv_sem=recv_sems.at[c, p - 1],
            device_id={"gx": target},
            device_id_type=MESH,
        )

    def send(c):
        for p in order:
            outgoing(c, p).start()

    enter(n, me)
    for c in range(min(WINDOW, chunks)):
        send(jnp.int32(c))
    own = pltpu.make_async_copy(
        demand.at[pl.ds(me * layers, layers)],
        regrouped.at[:, pl.ds(pl.multiple_of(me * rows, rows), rows), :],
        self_sem,
    )
    own.start()
    gram[...] = jnp.zeros_like(gram)
    own.wait()
    tiles = gram.shape[0] // TILE

    def step(c, carry):
        @pl.when(c + WINDOW < chunks)
        def _():
            send(c + WINDOW)

        for p in order:
            outgoing(c, p).wait_recv()
        layer, column = place(c)
        load = pltpu.make_async_copy(regrouped.at[layer, :, pl.ds(column, width)], block, load_sem)
        load.start()
        load.wait()

        @pl.loop(0, tiles)
        def _(i):
            first = pl.ds(pl.multiple_of(i * TILE, TILE), TILE)

            @pl.loop(i, tiles)
            def _(j):
                second = pl.ds(pl.multiple_of(j * TILE, TILE), TILE)
                gram[first, second] += dot(block[first, :], block[second, :], ((1,), (1,)))

        return carry

    lax.fori_loop(0, chunks, step, 0)

    def finish(c, carry):
        for p in order:
            outgoing(c, p).wait_send()
        return carry

    lax.fori_loop(0, chunks, finish, 0)

    @pl.loop(0, tiles)
    def _(i):
        first = pl.ds(pl.multiple_of(i * TILE, TILE), TILE)
        gram[first, first] = gram[first, first] * scale

        @pl.loop(i + 1, tiles)
        def _(j):
            second = pl.ds(pl.multiple_of(j * TILE, TILE), TILE)
            part = gram[first, second] * scale
            gram[first, second] = part
            gram[second, first] = part.T


def exchange_gram(demand, n, scale):
    total_layers, rows, columns = demand.shape
    layers = total_layers // n
    width = chunk_columns(layers, columns)
    chunks = layers * columns // width
    size = n * rows
    return pl.pallas_call(
        functools.partial(exchange_gram_kernel, n, layers, width, scale),
        out_shape=(
            jax.ShapeDtypeStruct((layers, size, columns), jnp.float32),
            jax.ShapeDtypeStruct((size, size), jnp.float32),
        ),
        in_specs=[pl.BlockSpec(memory_space=pl.ANY)],
        out_specs=(pl.BlockSpec(memory_space=pl.ANY), pl.BlockSpec(memory_space=pltpu.VMEM)),
        scratch_shapes=[
            pltpu.VMEM((size, width), jnp.float32),
            pltpu.SemaphoreType.DMA((chunks, n - 1)),
            pltpu.SemaphoreType.DMA((chunks, n - 1)),
            pltpu.SemaphoreType.DMA,
            pltpu.SemaphoreType.DMA,
        ],
        compiler_params=pltpu.CompilerParams(
            collective_id=0, has_side_effects=True, vmem_limit_bytes=40 * 2**20
        ),
        name="exchange_gram",
    )(demand)


def iterate_kernel(gram, initial, basis, image, work, inverse):
    size, rank = initial.shape
    lanes = 128
    basis[...] = initial[...]
    tiles = size // TILE

    def iteration(step, carry):
        work[:, :rank] = jnp.zeros((rank, rank), jnp.float32)

        @pl.loop(0, tiles)
        def _(i):
            rows = pl.ds(pl.multiple_of(i * TILE, TILE), TILE)
            part = dot(gram[rows, :], basis[...], ((1,), (0,)))
            image[rows, :] = part
            work[:, :rank] += dot(part, part, ((0,), (0,)))

        row = lax.broadcasted_iota(jnp.int32, (rank, rank), 0)
        column = lax.broadcasted_iota(jnp.int32, (rank, rank), 1)
        work[:, rank:] = (row == column).astype(jnp.float32)
        inverse[...] = jnp.zeros_like(inverse)
        index = lax.broadcasted_iota(jnp.int32, (PANEL, 1), 0)
        for k in range(0, rank, PANEL):
            low = k // lanes * lanes
            end = (k + PANEL - 1) // lanes * lanes + lanes
            panel = work[k : k + PANEL, low : rank + end]
            pivots = jnp.ones((PANEL, 1), jnp.float32)
            for j in range(PANEL):
                at = k + j - low
                pivot_column = panel[:, at : at + 1]
                pivot = pivot_column[j : j + 1, :]
                ratio = jnp.where(index > j, pivot_column / pivot, 0.0)
                pivots = jnp.where(index == j, pivot, pivots)
                panel = panel - ratio * panel[j : j + 1, :]
            panel = panel * (1.0 / jnp.sqrt(pivots))
            inverse[k : k + PANEL, :end] = panel[:, rank - low :]
            if k + PANEL < rank:
                update = dot(panel[:, : rank - low], panel, ((0,), (0,)))
                work[k + PANEL :, low : rank + end] -= update[k + PANEL - low :, :]

        @pl.loop(0, tiles)
        def _(i):
            rows = pl.ds(pl.multiple_of(i * TILE, TILE), TILE)
            basis[rows, :] = dot(image[rows, :], inverse[...], ((1,), (1,)))

        return carry

    lax.fori_loop(0, ITERS, iteration, 0)


def iterate(gram, initial):
    size, rank = initial.shape
    return pl.pallas_call(
        iterate_kernel,
        out_shape=jax.ShapeDtypeStruct((size, rank), jnp.float32),
        in_specs=[pl.BlockSpec(memory_space=pltpu.VMEM)] * 2,
        out_specs=pl.BlockSpec(memory_space=pltpu.VMEM),
        scratch_shapes=[
            pltpu.VMEM((size, rank), jnp.float32),
            pltpu.VMEM((rank, 2 * rank), jnp.float32),
            pltpu.VMEM((rank, rank), jnp.float32),
        ],
        compiler_params=pltpu.CompilerParams(vmem_limit_bytes=40 * 2**20),
        name="iterate",
    )(gram, initial)


def project_kernel(
    n, width, regrouped, basis, core, block, made, send_sems, recv_sems, self_sems, load_sems
):
    me = lax.axis_index("gx")
    layers, size, columns = regrouped.shape
    rank = basis.shape[1]
    share = rank // n
    per_layer = columns // width
    chunks = layers * per_layer
    order = far_first(n)

    def place(c):
        return lax.div(c, per_layer), pl.multiple_of(lax.rem(c, per_layer) * width, width)

    def load(c):
        layer, column = place(c)
        slot = lax.rem(c, 2)
        return pltpu.make_async_copy(
            regrouped.at[layer, :, pl.ds(column, width)], block.at[slot], load_sems.at[slot]
        )

    def outgoing(c, p):
        layer, column = place(c)
        target = lax.rem(me + p, n)
        return pltpu.make_async_remote_copy(
            src_ref=made.at[c, pl.ds(pl.multiple_of(target * share, share), share), :],
            dst_ref=core.at[me * layers + layer, :, pl.ds(column, width)],
            send_sem=send_sems.at[c, p - 1],
            recv_sem=recv_sems.at[c, p - 1],
            device_id={"gx": target},
            device_id_type=MESH,
        )

    def own(c):
        layer, column = place(c)
        return pltpu.make_async_copy(
            made.at[c, pl.ds(pl.multiple_of(me * share, share), share), :],
            core.at[me * layers + layer, :, pl.ds(column, width)],
            self_sems.at[c],
        )

    load(jnp.int32(0)).start()
    enter(n, me)

    def step(c, carry):
        slot = lax.rem(c, 2)

        @pl.when(c + 1 < chunks)
        def _():
            load(c + 1).start()

        load(c).wait()
        tile = min(width, TILE)

        @pl.loop(0, width // tile)
        def _(i):
            some = pl.ds(pl.multiple_of(i * tile, tile), tile)
            made[c, :, some] = dot(basis[...], block[slot, :, some], ((0,), (0,)))

        for p in order:
            outgoing(c, p).start()
        own(c).start()
        return carry

    lax.fori_loop(0, chunks, step, 0)

    def finish(c, carry):
        own(c).wait()
        for p in order:
            outgoing(c, p).wait()
        return carry

    lax.fori_loop(0, chunks, finish, 0)


def project(regrouped, basis, n):
    layers, size, columns = regrouped.shape
    rank = basis.shape[1]
    width = chunk_columns(layers, columns)
    chunks = layers * columns // width
    return pl.pallas_call(
        functools.partial(project_kernel, n, width),
        out_shape=jax.ShapeDtypeStruct((layers * n, rank // n, columns), jnp.float32),
        in_specs=[pl.BlockSpec(memory_space=pl.ANY), pl.BlockSpec(memory_space=pltpu.VMEM)],
        out_specs=pl.BlockSpec(memory_space=pl.ANY),
        scratch_shapes=[
            pltpu.VMEM((2, size, width), jnp.float32),
            pltpu.VMEM((chunks, rank, width), jnp.float32),
            pltpu.SemaphoreType.DMA((chunks, n - 1)),
            pltpu.SemaphoreType.DMA((chunks, n - 1)),
            pltpu.SemaphoreType.DMA((chunks,)),
            pltpu.SemaphoreType.DMA((2,)),
        ],
        compiler_params=pltpu.CompilerParams(
            collective_id=1, has_side_effects=True, vmem_limit_bytes=40 * 2**20
        ),
        name="project",
    )(regrouped, basis)


def on_device(n, groups, demand, initial):
    scale = 1.0 / (demand.shape[0] * demand.shape[2] * groups)
    regrouped, local_gram = exchange_gram(demand, n, scale)
    gram = lax.psum(local_gram, ("gx", "gy"))
    basis = iterate(gram, initial)
    core = project(regrouped, basis, n)
    return (basis, jnp.transpose(core, (1, 0, 2)))


def solution(mesh):
    in_specs = (P(None, "gx", "gy"), P())
    out_specs = (P(), P("gx", None, "gy"))
    return jax.shard_map(
        functools.partial(on_device, mesh.shape["gx"], mesh.shape["gy"]),
        mesh=mesh,
        in_specs=in_specs,
        out_specs=out_specs,
        check_vma=False,
    )
```

```python
import functools

import jax
import jax.numpy as jnp
from jax import lax
from jax.experimental import pallas as pl
from jax.experimental.pallas import tpu as pltpu
from jax.sharding import PartitionSpec as P

ITERS = 3
TILE = 256
PANEL = 32
GROUP = 8
WINDOW = 3
MESH = pl.DeviceIdType.MESH
HIGHEST = lax.Precision.HIGHEST


def dot(left, right, dims):
    return lax.dot_general(
        left, right, (dims, ((), ())), precision=HIGHEST, preferred_element_type=jnp.float32
    )


def chunk_columns(layers, columns):
    return min(columns, max(128, layers * columns // 8))


def far_first(n):
    return sorted(range(1, n), key=lambda p: (abs(p - n // 2), p))


def enter(n, me):
    barrier = pltpu.get_barrier_semaphore()
    for p in range(1, n):
        pl.semaphore_signal(
            barrier, inc=1, device_id={"gx": lax.rem(me + p, n)}, device_id_type=MESH
        )
    pl.semaphore_wait(barrier, n - 1)


def tile_row(tiles, i, j):
    return (i * tiles - lax.div(i * (i - 1), 2) + j - i) * TILE


def packed_rows(size, devices):
    tiles = size // TILE
    unit = 8 * devices
    return -(-(tiles * (tiles + 1) // 2 * TILE) // unit) * unit


def exchange_gram_kernel(
    n, layers, width, scale, demand, regrouped, gram, block, send_sems, recv_sems, self_sem, load_sem
):
    me = lax.axis_index("gx")
    rows, columns = demand.shape[1], demand.shape[2]
    per_layer = columns // width
    chunks = layers * per_layer
    order = far_first(n)

    def place(c):
        return lax.div(c, per_layer), pl.multiple_of(lax.rem(c, per_layer) * width, width)

    def outgoing(c, p):
        layer, column = place(c)
        target = lax.rem(me + p, n)
        return pltpu.make_async_remote_copy(
            src_ref=demand.at[target * layers + layer, :, pl.ds(column, width)],
            dst_ref=regrouped.at[layer, pl.ds(pl.multiple_of(me * rows, rows), rows), pl.ds(column, width)],
            send_sem=send_sems.at[c, p - 1],
            recv_sem=recv_sems.at[c, p - 1],
            device_id={"gx": target},
            device_id_type=MESH,
        )

    def send(c):
        for p in order:
            outgoing(c, p).start()

    enter(n, me)
    for c in range(min(WINDOW, chunks)):
        send(jnp.int32(c))
    own = pltpu.make_async_copy(
        demand.at[pl.ds(me * layers, layers)],
        regrouped.at[:, pl.ds(pl.multiple_of(me * rows, rows), rows), :],
        self_sem,
    )
    own.start()
    gram[...] = jnp.zeros_like(gram)
    own.wait()
    tiles = n * rows // TILE

    def step(c, carry):
        @pl.when(c + WINDOW < chunks)
        def _():
            send(c + WINDOW)

        for p in order:
            outgoing(c, p).wait_recv()
        layer, column = place(c)
        load = pltpu.make_async_copy(regrouped.at[layer, :, pl.ds(column, width)], block, load_sem)
        load.start()
        load.wait()

        @pl.loop(0, tiles)
        def _(i):
            first = pl.ds(pl.multiple_of(i * TILE, TILE), TILE)

            @pl.loop(i, tiles)
            def _(j):
                second = pl.ds(pl.multiple_of(j * TILE, TILE), TILE)
                packed = pl.ds(pl.multiple_of(tile_row(tiles, i, j), TILE), TILE)
                gram[packed, :] += dot(block[first, :], block[second, :], ((1,), (1,)))

        return carry

    lax.fori_loop(0, chunks, step, 0)

    def finish(c, carry):
        for p in order:
            outgoing(c, p).wait_send()
        return carry

    lax.fori_loop(0, chunks, finish, 0)
    gram[...] = gram[...] * scale


def exchange_gram(demand, n, groups, scale):
    total_layers, rows, columns = demand.shape
    layers = total_layers // n
    width = chunk_columns(layers, columns)
    chunks = layers * columns // width
    size = n * rows
    return pl.pallas_call(
        functools.partial(exchange_gram_kernel, n, layers, width, scale),
        out_shape=(
            jax.ShapeDtypeStruct((layers, size, columns), jnp.float32),
            jax.ShapeDtypeStruct((packed_rows(size, n * groups), TILE), jnp.float32),
        ),
        in_specs=[pl.BlockSpec(memory_space=pl.ANY)],
        out_specs=(pl.BlockSpec(memory_space=pl.ANY), pl.BlockSpec(memory_space=pltpu.VMEM)),
        scratch_shapes=[
            pltpu.VMEM((size, width), jnp.float32),
            pltpu.SemaphoreType.DMA((chunks, n - 1)),
            pltpu.SemaphoreType.DMA((chunks, n - 1)),
            pltpu.SemaphoreType.DMA,
            pltpu.SemaphoreType.DMA,
        ],
        compiler_params=pltpu.CompilerParams(
            collective_id=0, has_side_effects=True, vmem_limit_bytes=40 * 2**20
        ),
        name="exchange_gram",
    )(demand)


def sum_gram_kernel(
    n, groups, local, out, total, half_in, half, quarter_in, quarter, piece_in, send_sems, recv_sems
):
    me = lax.axis_index("gx")
    group = lax.axis_index("gy")
    z, core = lax.div(me, 2), lax.rem(me, 2)
    depth = n // 2
    mate = me + 1 - 2 * core
    half_rows = local.shape[0] // 2
    quarter_rows = half_rows // groups
    piece_rows = quarter_rows // depth

    def copy(src, dst, slot, device):
        return pltpu.make_async_remote_copy(
            src_ref=src,
            dst_ref=dst,
            send_sem=send_sems.at[slot],
            recv_sem=recv_sems.at[slot],
            device_id=device,
            device_id_type=MESH,
        )

    def rows(start, count):
        return pl.ds(pl.multiple_of(start, 8), count)

    def along_gy(q):
        return lax.rem(group + q, groups)

    def along_z(q):
        return lax.rem(z + q, depth)

    def gy_device(q):
        return {"gx": me, "gy": along_gy(q)}

    def z_device(q):
        return {"gx": along_z(q) * 2 + core, "gy": group}

    mate_device = {"gx": mate, "gy": group}
    barrier = pltpu.get_barrier_semaphore()
    near = [mate_device]
    near += [gy_device(q) for q in range(1, groups)]
    near += [z_device(q) for q in range(1, depth)]
    for device in near:
        pl.semaphore_signal(barrier, inc=1, device_id=device, device_id_type=MESH)
    pl.semaphore_wait(barrier, len(near))

    first = copy(local.at[rows((1 - core) * half_rows, half_rows)], half_in, 0, mate_device)
    first.start()
    first.wait()
    half[...] = local[rows(core * half_rows, half_rows), :] + half_in[...]
    slot = 1
    seconds = []
    for q in range(1, groups):
        part = half.at[rows(along_gy(q) * quarter_rows, quarter_rows)]
        seconds.append(copy(part, quarter_in.at[q - 1], slot, gy_device(q)))
        seconds[-1].start()
        slot += 1
    value = half[rows(group * quarter_rows, quarter_rows), :]
    for q in range(1, groups):
        seconds[q - 1].wait()
        value = value + quarter_in[q - 1]
    quarter[...] = value
    thirds = []
    for q in range(1, depth):
        part = quarter.at[rows(along_z(q) * piece_rows, piece_rows)]
        thirds.append(copy(part, piece_in.at[q - 1], slot, z_device(q)))
        thirds[-1].start()
        slot += 1
    value = quarter[rows(z * piece_rows, piece_rows), :]
    for q in range(1, depth):
        thirds[q - 1].wait()
        value = value + piece_in[q - 1]

    base = core * half_rows
    mine = base + group * quarter_rows
    total[rows(mine + z * piece_rows, piece_rows), :] = value
    piece = total.at[rows(mine + z * piece_rows, piece_rows)]
    fourths = []
    for q in range(1, depth):
        fourths.append(copy(piece, piece, slot, z_device(q)))
        fourths[-1].start()
        slot += 1
    for done in fourths:
        done.wait()
    own_quarter = total.at[rows(mine, quarter_rows)]
    fifths = []
    for q in range(1, groups):
        fifths.append(copy(own_quarter, own_quarter, slot, gy_device(q)))
        fifths[-1].start()
        slot += 1
    lasts = [copy(own_quarter, own_quarter, slot, mate_device)]
    lasts[0].start()
    slot += 1
    for q in range(1, groups):
        fifths[q - 1].wait()
        source = lax.rem(group + groups - q, groups)
        part = total.at[rows(base + source * quarter_rows, quarter_rows)]
        lasts.append(copy(part, part, slot, mate_device))
        lasts[-1].start()
        slot += 1
    for done in lasts:
        done.wait()
    out[...] = total[...]


def sum_gram(local, n, groups):
    rows, lanes = local.shape
    half, quarter, piece = rows // 2, rows // 2 // groups, rows // n // groups
    copies = 1 + 2 * (groups - 1) + 2 * (n // 2 - 1) + groups
    return pl.pallas_call(
        functools.partial(sum_gram_kernel, n, groups),
        out_shape=jax.ShapeDtypeStruct((rows, lanes), jnp.float32),
        in_specs=[pl.BlockSpec(memory_space=pltpu.VMEM)],
        out_specs=pl.BlockSpec(memory_space=pltpu.VMEM),
        scratch_shapes=[
            pltpu.VMEM((rows, lanes), jnp.float32),
            pltpu.VMEM((half, lanes), jnp.float32),
            pltpu.VMEM((half, lanes), jnp.float32),
            pltpu.VMEM((groups - 1, quarter, lanes), jnp.float32),
            pltpu.VMEM((quarter, lanes), jnp.float32),
            pltpu.VMEM((n // 2 - 1, piece, lanes), jnp.float32),
            pltpu.SemaphoreType.DMA((copies,)),
            pltpu.SemaphoreType.DMA((copies,)),
        ],
        compiler_params=pltpu.CompilerParams(
            collective_id=2, has_side_effects=True, vmem_limit_bytes=40 * 2**20
        ),
        name="sum_gram",
    )(local)


def iterate_kernel(packed, initial, basis, gram, image, work, inverse):
    size, rank = initial.shape
    lanes = 128
    basis[...] = initial[...]
    tiles = size // TILE

    @pl.loop(0, tiles)
    def _(i):
        first = pl.ds(pl.multiple_of(i * TILE, TILE), TILE)
        diagonal = pl.ds(pl.multiple_of(tile_row(tiles, i, i), TILE), TILE)
        gram[first, first] = packed[diagonal, :]

        @pl.loop(i + 1, tiles)
        def _(j):
            second = pl.ds(pl.multiple_of(j * TILE, TILE), TILE)
            part = packed[pl.ds(pl.multiple_of(tile_row(tiles, i, j), TILE), TILE), :]
            gram[first, second] = part
            gram[second, first] = part.T

    def iteration(step, carry):
        work[:, :rank] = jnp.zeros((rank, rank), jnp.float32)

        @pl.loop(0, tiles)
        def _(i):
            rows = pl.ds(pl.multiple_of(i * TILE, TILE), TILE)
            part = dot(gram[rows, :], basis[...], ((1,), (0,)))
            image[rows, :] = part
            work[:, :rank] += dot(part, part, ((0,), (0,)))

        row = lax.broadcasted_iota(jnp.int32, (rank, rank), 0)
        column = lax.broadcasted_iota(jnp.int32, (rank, rank), 1)
        work[:, rank:] = (row == column).astype(jnp.float32)
        inverse[...] = jnp.zeros_like(inverse)
        index = lax.broadcasted_iota(jnp.int32, (PANEL, lanes), 0)
        for k in range(0, rank, PANEL):
            low = k // lanes * lanes
            end = (k + PANEL - 1) // lanes * lanes + lanes
            strips = [
                work[k : k + PANEL, at : at + lanes] for at in range(low, rank + end, lanes)
            ]
            pivots = jnp.ones((PANEL, lanes), jnp.float32)
            for start in range(0, PANEL, GROUP):
                ahead = []
                for j in range(start, start + GROUP):
                    strip, at = divmod(k + j - low, lanes)
                    ahead.append(
                        jnp.broadcast_to(strips[strip][:, at : at + 1], (PANEL, lanes))
                    )
                for j in range(start, start + GROUP):
                    current = ahead[j - start]
                    pivot = current[j : j + 1, :]
                    ratio = jnp.where(index > j, current * (1.0 / pivot), 0.0)
                    pivots = jnp.where(index == j, pivot, pivots)
                    for t in range(j - start + 1, GROUP):
                        ahead[t] = ahead[t] - ratio * ahead[t][j : j + 1, :]
                    strips = [strip - ratio * strip[j : j + 1, :] for strip in strips]
            root = 1.0 / jnp.sqrt(pivots)
            panel = jnp.concatenate([strip * root for strip in strips], axis=1)
            inverse[k : k + PANEL, :end] = panel[:, rank - low :]
            if k + PANEL < rank:
                update = dot(panel[:, : rank - low], panel, ((0,), (0,)))
                work[k + PANEL :, low : rank + end] -= update[k + PANEL - low :, :]

        @pl.loop(0, tiles)
        def _(i):
            rows = pl.ds(pl.multiple_of(i * TILE, TILE), TILE)
            basis[rows, :] = dot(image[rows, :], inverse[...], ((1,), (1,)))

        return carry

    lax.fori_loop(0, ITERS, iteration, 0)


def iterate(packed, initial):
    size, rank = initial.shape
    return pl.pallas_call(
        iterate_kernel,
        out_shape=jax.ShapeDtypeStruct((size, rank), jnp.float32),
        in_specs=[pl.BlockSpec(memory_space=pltpu.VMEM)] * 2,
        out_specs=pl.BlockSpec(memory_space=pltpu.VMEM),
        scratch_shapes=[
            pltpu.VMEM((size, size), jnp.float32),
            pltpu.VMEM((size, rank), jnp.float32),
            pltpu.VMEM((rank, 2 * rank), jnp.float32),
            pltpu.VMEM((rank, rank), jnp.float32),
        ],
        compiler_params=pltpu.CompilerParams(vmem_limit_bytes=40 * 2**20),
        name="iterate",
    )(packed, initial)


def project_kernel(
    n, width, regrouped, basis, core, block, made, send_sems, recv_sems, self_sems, load_sems
):
    me = lax.axis_index("gx")
    layers, size, columns = regrouped.shape
    rank = basis.shape[1]
    share = rank // n
    per_layer = columns // width
    chunks = layers * per_layer
    order = far_first(n)

    def place(c):
        return lax.div(c, per_layer), pl.multiple_of(lax.rem(c, per_layer) * width, width)

    def load(c):
        layer, column = place(c)
        slot = lax.rem(c, 2)
        return pltpu.make_async_copy(
            regrouped.at[layer, :, pl.ds(column, width)], block.at[slot], load_sems.at[slot]
        )

    def outgoing(c, p):
        layer, column = place(c)
        target = lax.rem(me + p, n)
        return pltpu.make_async_remote_copy(
            src_ref=made.at[c, pl.ds(pl.multiple_of(target * share, share), share), :],
            dst_ref=core.at[me * layers + layer, :, pl.ds(column, width)],
            send_sem=send_sems.at[c, p - 1],
            recv_sem=recv_sems.at[c, p - 1],
            device_id={"gx": target},
            device_id_type=MESH,
        )

    def own(c):
        layer, column = place(c)
        return pltpu.make_async_copy(
            made.at[c, pl.ds(pl.multiple_of(me * share, share), share), :],
            core.at[me * layers + layer, :, pl.ds(column, width)],
            self_sems.at[c],
        )

    load(jnp.int32(0)).start()
    enter(n, me)

    def step(c, carry):
        slot = lax.rem(c, 2)

        @pl.when(c + 1 < chunks)
        def _():
            load(c + 1).start()

        load(c).wait()
        tile = min(width, TILE)

        @pl.loop(0, width // tile)
        def _(i):
            some = pl.ds(pl.multiple_of(i * tile, tile), tile)
            made[c, :, some] = dot(basis[...], block[slot, :, some], ((0,), (0,)))

        for p in order:
            outgoing(c, p).start()
        own(c).start()
        return carry

    lax.fori_loop(0, chunks, step, 0)

    def finish(c, carry):
        own(c).wait()
        for p in order:
            outgoing(c, p).wait()
        return carry

    lax.fori_loop(0, chunks, finish, 0)


def project(regrouped, basis, n):
    layers, size, columns = regrouped.shape
    rank = basis.shape[1]
    width = chunk_columns(layers, columns)
    chunks = layers * columns // width
    return pl.pallas_call(
        functools.partial(project_kernel, n, width),
        out_shape=jax.ShapeDtypeStruct((layers * n, rank // n, columns), jnp.float32),
        in_specs=[pl.BlockSpec(memory_space=pl.ANY), pl.BlockSpec(memory_space=pltpu.VMEM)],
        out_specs=pl.BlockSpec(memory_space=pl.ANY),
        scratch_shapes=[
            pltpu.VMEM((2, size, width), jnp.float32),
            pltpu.VMEM((chunks, rank, width), jnp.float32),
            pltpu.SemaphoreType.DMA((chunks, n - 1)),
            pltpu.SemaphoreType.DMA((chunks, n - 1)),
            pltpu.SemaphoreType.DMA((chunks,)),
            pltpu.SemaphoreType.DMA((2,)),
        ],
        compiler_params=pltpu.CompilerParams(
            collective_id=1, has_side_effects=True, vmem_limit_bytes=40 * 2**20
        ),
        name="project",
    )(regrouped, basis)


def on_device(n, groups, demand, initial):
    scale = 1.0 / (demand.shape[0] * demand.shape[2] * groups)
    regrouped, local_gram = exchange_gram(demand, n, groups, scale)
    basis = iterate(sum_gram(local_gram, n, groups), initial)
    core = project(regrouped, basis, n)
    return (basis, jnp.transpose(core, (1, 0, 2)))


def solution(mesh):
    in_specs = (P(None, "gx", "gy"), P())
    out_specs = (P(), P("gx", None, "gy"))
    return jax.shard_map(
        functools.partial(on_device, mesh.shape["gx"], mesh.shape["gy"]),
        mesh=mesh,
        in_specs=in_specs,
        out_specs=out_specs,
        check_vma=False,
    )
```

```python
import functools

import jax
import jax.numpy as jnp
from jax import lax
from jax.experimental import pallas as pl
from jax.experimental.pallas import tpu as pltpu
from jax.sharding import PartitionSpec as P

ITERS = 3
TILE = 256
PANEL = 32
GROUP = 8
WINDOW = 6
MESH = pl.DeviceIdType.MESH
HIGHEST = lax.Precision.HIGHEST


def dot(left, right, dims):
    return lax.dot_general(
        left, right, (dims, ((), ())), precision=HIGHEST, preferred_element_type=jnp.float32
    )


def chunk_columns(layers, columns):
    return min(columns, max(128, layers * columns // 16))


def far_first(n):
    return sorted(range(1, n), key=lambda p: (abs(p - n // 2), p))


def enter(n, me):
    barrier = pltpu.get_barrier_semaphore()
    for p in range(1, n):
        pl.semaphore_signal(
            barrier, inc=1, device_id={"gx": lax.rem(me + p, n)}, device_id_type=MESH
        )
    pl.semaphore_wait(barrier, n - 1)


def tile_row(tiles, i, j):
    return (i * tiles - lax.div(i * (i - 1), 2) + j - i) * TILE


def packed_rows(size, devices):
    tiles = size // TILE
    unit = 16 * devices
    return -(-(tiles * (tiles + 1) // 2 * TILE) // unit) * unit


def exchange_gram_kernel(
    n, layers, width, scale, demand, regrouped, gram, block, send_sems, recv_sems, self_sem, load_sem
):
    me = lax.axis_index("gx")
    rows, columns = demand.shape[1], demand.shape[2]
    per_layer = columns // width
    chunks = layers * per_layer
    order = far_first(n)

    def place(c):
        return lax.div(c, per_layer), pl.multiple_of(lax.rem(c, per_layer) * width, width)

    def outgoing(c, p):
        layer, column = place(c)
        target = lax.rem(me + p, n)
        return pltpu.make_async_remote_copy(
            src_ref=demand.at[target * layers + layer, :, pl.ds(column, width)],
            dst_ref=regrouped.at[layer, pl.ds(pl.multiple_of(me * rows, rows), rows), pl.ds(column, width)],
            send_sem=send_sems.at[c, p - 1],
            recv_sem=recv_sems.at[c, p - 1],
            device_id={"gx": target},
            device_id_type=MESH,
        )

    def send(c):
        for p in order:
            outgoing(c, p).start()

    enter(n, me)
    for c in range(min(WINDOW, chunks)):
        send(jnp.int32(c))
    own = pltpu.make_async_copy(
        demand.at[pl.ds(me * layers, layers)],
        regrouped.at[:, pl.ds(pl.multiple_of(me * rows, rows), rows), :],
        self_sem,
    )
    own.start()
    gram[...] = jnp.zeros_like(gram)
    own.wait()
    tiles = n * rows // TILE

    def step(c, carry):
        @pl.when(c + WINDOW < chunks)
        def _():
            send(c + WINDOW)

        for p in order:
            outgoing(c, p).wait_recv()
        layer, column = place(c)
        load = pltpu.make_async_copy(regrouped.at[layer, :, pl.ds(column, width)], block, load_sem)
        load.start()
        load.wait()

        @pl.loop(0, tiles)
        def _(i):
            first = pl.ds(pl.multiple_of(i * TILE, TILE), TILE)

            @pl.loop(i, tiles)
            def _(j):
                second = pl.ds(pl.multiple_of(j * TILE, TILE), TILE)
                packed = pl.ds(pl.multiple_of(tile_row(tiles, i, j), TILE), TILE)
                gram[packed, :] += dot(block[first, :], block[second, :], ((1,), (1,)))

        return carry

    lax.fori_loop(0, chunks, step, 0)

    def finish(c, carry):
        for p in order:
            outgoing(c, p).wait_send()
        return carry

    lax.fori_loop(0, chunks, finish, 0)
    gram[...] = gram[...] * scale


def exchange_gram(demand, n, groups, scale):
    total_layers, rows, columns = demand.shape
    layers = total_layers // n
    width = chunk_columns(layers, columns)
    chunks = layers * columns // width
    size = n * rows
    return pl.pallas_call(
        functools.partial(exchange_gram_kernel, n, layers, width, scale),
        out_shape=(
            jax.ShapeDtypeStruct((layers, size, columns), jnp.float32),
            jax.ShapeDtypeStruct((packed_rows(size, n * groups), TILE), jnp.float32),
        ),
        in_specs=[pl.BlockSpec(memory_space=pl.ANY)],
        out_specs=(pl.BlockSpec(memory_space=pl.ANY), pl.BlockSpec(memory_space=pltpu.VMEM)),
        scratch_shapes=[
            pltpu.VMEM((size, width), jnp.float32),
            pltpu.SemaphoreType.DMA((chunks, n - 1)),
            pltpu.SemaphoreType.DMA((chunks, n - 1)),
            pltpu.SemaphoreType.DMA,
            pltpu.SemaphoreType.DMA,
        ],
        compiler_params=pltpu.CompilerParams(
            collective_id=0, has_side_effects=True, vmem_limit_bytes=40 * 2**20
        ),
        name="exchange_gram",
    )(demand)


def sum_gram_kernel(
    n, groups, local, out, total, half_in, half, gy_wide, z_narrow, z_wide, gy_narrow,
    middle_gy, middle_z, send_sems, recv_sems
):
    me = lax.axis_index("gx")
    group = lax.axis_index("gy")
    z, core = lax.div(me, 2), lax.rem(me, 2)
    depth = n // 2
    mate = me + 1 - 2 * core
    half_rows = local.shape[0] // 2
    track_rows = half_rows // 2
    piece_rows = track_rows // groups // depth
    used = [0]

    def copy(src, dst, device):
        slot = used[0]
        used[0] += 1
        started = pltpu.make_async_remote_copy(
            src_ref=src,
            dst_ref=dst,
            send_sem=send_sems.at[slot],
            recv_sem=recv_sems.at[slot],
            device_id=device,
            device_id_type=MESH,
        )
        started.start()
        return started

    def rows(start, count):
        return pl.ds(pl.multiple_of(start, 8), count)

    def along_gy(q):
        return lax.rem(group + q, groups)

    def along_z(q):
        return lax.rem(z + q, depth)

    def gy_device(q):
        return {"gx": me, "gy": along_gy(q)}

    def z_device(q):
        return {"gx": along_z(q) * 2 + core, "gy": group}

    mate_device = {"gx": mate, "gy": group}
    barrier = pltpu.get_barrier_semaphore()
    near = [mate_device]
    near += [gy_device(q) for q in range(1, groups)]
    near += [z_device(q) for q in range(1, depth)]
    for device in near:
        pl.semaphore_signal(barrier, inc=1, device_id=device, device_id_type=MESH)
    pl.semaphore_wait(barrier, len(near))

    gy_axis = (groups, group, along_gy, gy_device)
    z_axis = (depth, z, along_z, z_device)

    def scatter(source, offset, count, landing, axis):
        size, _, along, device = axis
        part = count // size
        return [
            copy(source.at[rows(offset + along(q) * part, part)], landing.at[q - 1], device(q))
            for q in range(1, size)
        ]

    def collect(copies, source, offset, count, landing, axis):
        size, here, _, _ = axis
        part = count // size
        value = source[rows(offset + here * part, part), :]
        for q in range(1, size):
            copies[q - 1].wait()
            value = value + landing[q - 1]
        return value

    def spread(start, count, axis):
        part = total.at[rows(start, count)]
        return [copy(part, part, axis[3](q)) for q in range(1, axis[0])]

    def wait(copies):
        for done in copies:
            done.wait()

    first = copy(local.at[rows((1 - core) * half_rows, half_rows)], half_in, mate_device)
    first.wait()
    half[...] = local[rows(core * half_rows, half_rows), :] + half_in[...]
    wide_a = scatter(half, 0, track_rows, gy_wide, gy_axis)
    wide_b = scatter(half, track_rows, track_rows, z_wide, z_axis)
    gy_rows, z_rows = track_rows // groups, track_rows // depth
    middle_gy[...] = collect(wide_a, half, 0, track_rows, gy_wide, gy_axis)
    narrow_a = scatter(middle_gy, 0, gy_rows, z_narrow, z_axis)
    middle_z[...] = collect(wide_b, half, track_rows, track_rows, z_wide, z_axis)
    narrow_b = scatter(middle_z, 0, z_rows, gy_narrow, gy_axis)

    base_a = core * half_rows
    base_b = base_a + track_rows
    part_a = base_a + group * gy_rows
    part_b = base_b + z * z_rows
    piece_a = part_a + z * piece_rows
    piece_b = part_b + group * piece_rows
    total[rows(piece_a, piece_rows), :] = collect(
        narrow_a, middle_gy, 0, gy_rows, z_narrow, z_axis
    )
    back_a = spread(piece_a, piece_rows, z_axis)
    total[rows(piece_b, piece_rows), :] = collect(
        narrow_b, middle_z, 0, z_rows, gy_narrow, gy_axis
    )
    back_b = spread(piece_b, piece_rows, gy_axis)
    wait(back_a)
    wide_a = spread(part_a, gy_rows, gy_axis)
    mine_a = total.at[rows(part_a, gy_rows)]
    lasts = [copy(mine_a, mine_a, mate_device)]
    wait(back_b)
    wide_b = spread(part_b, z_rows, z_axis)
    mine_b = total.at[rows(part_b, z_rows)]
    lasts.append(copy(mine_b, mine_b, mate_device))

    def hand_on(copies, base, count, axis):
        size, here, _, _ = axis
        for q in range(1, size):
            copies[q - 1].wait()
            source = lax.rem(here + size - q, size)
            part = total.at[rows(base + source * count, count)]
            lasts.append(copy(part, part, mate_device))

    hand_on(wide_a, base_a, gy_rows, gy_axis)
    hand_on(wide_b, base_b, z_rows, z_axis)
    wait(lasts)
    out[...] = total[...]


def sum_gram(local, n, groups):
    rows, lanes = local.shape
    depth = n // 2
    half, track = rows // 2, rows // 4
    piece = track // groups // depth
    copies = 1 + 4 * (groups - 1) + 4 * (depth - 1) + groups + depth
    return pl.pallas_call(
        functools.partial(sum_gram_kernel, n, groups),
        out_shape=jax.ShapeDtypeStruct((rows, lanes), jnp.float32),
        in_specs=[pl.BlockSpec(memory_space=pltpu.VMEM)],
        out_specs=pl.BlockSpec(memory_space=pltpu.VMEM),
        scratch_shapes=[
            pltpu.VMEM((rows, lanes), jnp.float32),
            pltpu.VMEM((half, lanes), jnp.float32),
            pltpu.VMEM((half, lanes), jnp.float32),
            pltpu.VMEM((groups - 1, track // groups, lanes), jnp.float32),
            pltpu.VMEM((depth - 1, piece, lanes), jnp.float32),
            pltpu.VMEM((depth - 1, track // depth, lanes), jnp.float32),
            pltpu.VMEM((groups - 1, piece, lanes), jnp.float32),
            pltpu.VMEM((track // groups, lanes), jnp.float32),
            pltpu.VMEM((track // depth, lanes), jnp.float32),
            pltpu.SemaphoreType.DMA((copies,)),
            pltpu.SemaphoreType.DMA((copies,)),
        ],
        compiler_params=pltpu.CompilerParams(
            collective_id=2, has_side_effects=True, vmem_limit_bytes=40 * 2**20
        ),
        name="sum_gram",
    )(local)


def iterate_kernel(packed, initial, basis, gram, image, work, inverse):
    size, rank = initial.shape
    lanes = 128
    basis[...] = initial[...]
    tiles = size // TILE

    @pl.loop(0, tiles)
    def _(i):
        first = pl.ds(pl.multiple_of(i * TILE, TILE), TILE)
        diagonal = pl.ds(pl.multiple_of(tile_row(tiles, i, i), TILE), TILE)
        gram[first, first] = packed[diagonal, :]

        @pl.loop(i + 1, tiles)
        def _(j):
            second = pl.ds(pl.multiple_of(j * TILE, TILE), TILE)
            part = packed[pl.ds(pl.multiple_of(tile_row(tiles, i, j), TILE), TILE), :]
            gram[first, second] = part
            gram[second, first] = part.T

    def iteration(step, carry):
        work[:, :rank] = jnp.zeros((rank, rank), jnp.float32)

        @pl.loop(0, tiles)
        def _(i):
            rows = pl.ds(pl.multiple_of(i * TILE, TILE), TILE)
            part = dot(gram[rows, :], basis[...], ((1,), (0,)))
            image[rows, :] = part
            work[:, :rank] += dot(part, part, ((0,), (0,)))

        row = lax.broadcasted_iota(jnp.int32, (rank, rank), 0)
        column = lax.broadcasted_iota(jnp.int32, (rank, rank), 1)
        work[:, rank:] = (row == column).astype(jnp.float32)
        inverse[...] = jnp.zeros_like(inverse)
        index = lax.broadcasted_iota(jnp.int32, (PANEL, lanes), 0)
        for k in range(0, rank, PANEL):
            low = k // lanes * lanes
            end = (k + PANEL - 1) // lanes * lanes + lanes
            strips = [
                work[k : k + PANEL, at : at + lanes] for at in range(low, rank + end, lanes)
            ]
            pivots = jnp.ones((PANEL, lanes), jnp.float32)
            for start in range(0, PANEL, GROUP):
                ahead = []
                for j in range(start, start + GROUP):
                    strip, at = divmod(k + j - low, lanes)
                    ahead.append(
                        jnp.broadcast_to(strips[strip][:, at : at + 1], (PANEL, lanes))
                    )
                for j in range(start, start + GROUP):
                    current = ahead[j - start]
                    pivot = current[j : j + 1, :]
                    ratio = jnp.where(index > j, current * (1.0 / pivot), 0.0)
                    pivots = jnp.where(index == j, pivot, pivots)
                    for t in range(j - start + 1, GROUP):
                        ahead[t] = ahead[t] - ratio * ahead[t][j : j + 1, :]
                    strips = [strip - ratio * strip[j : j + 1, :] for strip in strips]
            root = 1.0 / jnp.sqrt(pivots)
            panel = jnp.concatenate([strip * root for strip in strips], axis=1)
            inverse[k : k + PANEL, :end] = panel[:, rank - low :]
            if k + PANEL < rank:
                update = dot(panel[:, : rank - low], panel, ((0,), (0,)))
                work[k + PANEL :, low : rank + end] -= update[k + PANEL - low :, :]

        @pl.loop(0, tiles)
        def _(i):
            rows = pl.ds(pl.multiple_of(i * TILE, TILE), TILE)
            basis[rows, :] = dot(image[rows, :], inverse[...], ((1,), (1,)))

        return carry

    lax.fori_loop(0, ITERS, iteration, 0)


def iterate(packed, initial):
    size, rank = initial.shape
    return pl.pallas_call(
        iterate_kernel,
        out_shape=jax.ShapeDtypeStruct((size, rank), jnp.float32),
        in_specs=[pl.BlockSpec(memory_space=pltpu.VMEM)] * 2,
        out_specs=pl.BlockSpec(memory_space=pltpu.VMEM),
        scratch_shapes=[
            pltpu.VMEM((size, size), jnp.float32),
            pltpu.VMEM((size, rank), jnp.float32),
            pltpu.VMEM((rank, 2 * rank), jnp.float32),
            pltpu.VMEM((rank, rank), jnp.float32),
        ],
        compiler_params=pltpu.CompilerParams(vmem_limit_bytes=40 * 2**20),
        name="iterate",
    )(packed, initial)


def project_kernel(
    n, width, regrouped, basis, core, block, made, send_sems, recv_sems, self_sems, load_sems
):
    me = lax.axis_index("gx")
    layers, size, columns = regrouped.shape
    rank = basis.shape[1]
    share = rank // n
    per_layer = columns // width
    chunks = layers * per_layer
    order = far_first(n)

    def place(c):
        return lax.div(c, per_layer), pl.multiple_of(lax.rem(c, per_layer) * width, width)

    def load(c):
        layer, column = place(c)
        slot = lax.rem(c, 2)
        return pltpu.make_async_copy(
            regrouped.at[layer, :, pl.ds(column, width)], block.at[slot], load_sems.at[slot]
        )

    def outgoing(c, p):
        layer, column = place(c)
        target = lax.rem(me + p, n)
        return pltpu.make_async_remote_copy(
            src_ref=made.at[c, pl.ds(pl.multiple_of(target * share, share), share), :],
            dst_ref=core.at[me * layers + layer, :, pl.ds(column, width)],
            send_sem=send_sems.at[c, p - 1],
            recv_sem=recv_sems.at[c, p - 1],
            device_id={"gx": target},
            device_id_type=MESH,
        )

    def own(c):
        layer, column = place(c)
        return pltpu.make_async_copy(
            made.at[c, pl.ds(pl.multiple_of(me * share, share), share), :],
            core.at[me * layers + layer, :, pl.ds(column, width)],
            self_sems.at[c],
        )

    load(jnp.int32(0)).start()
    enter(n, me)

    def step(c, carry):
        slot = lax.rem(c, 2)

        @pl.when(c + 1 < chunks)
        def _():
            load(c + 1).start()

        load(c).wait()
        tile = min(width, TILE)

        @pl.loop(0, width // tile)
        def _(i):
            some = pl.ds(pl.multiple_of(i * tile, tile), tile)
            made[c, :, some] = dot(basis[...], block[slot, :, some], ((0,), (0,)))

        for p in order:
            outgoing(c, p).start()
        own(c).start()
        return carry

    lax.fori_loop(0, chunks, step, 0)

    def finish(c, carry):
        own(c).wait()
        for p in order:
            outgoing(c, p).wait()
        return carry

    lax.fori_loop(0, chunks, finish, 0)


def project(regrouped, basis, n):
    layers, size, columns = regrouped.shape
    rank = basis.shape[1]
    width = chunk_columns(layers, columns)
    chunks = layers * columns // width
    return pl.pallas_call(
        functools.partial(project_kernel, n, width),
        out_shape=jax.ShapeDtypeStruct((layers * n, rank // n, columns), jnp.float32),
        in_specs=[pl.BlockSpec(memory_space=pl.ANY), pl.BlockSpec(memory_space=pltpu.VMEM)],
        out_specs=pl.BlockSpec(memory_space=pl.ANY),
        scratch_shapes=[
            pltpu.VMEM((2, size, width), jnp.float32),
            pltpu.VMEM((chunks, rank, width), jnp.float32),
            pltpu.SemaphoreType.DMA((chunks, n - 1)),
            pltpu.SemaphoreType.DMA((chunks, n - 1)),
            pltpu.SemaphoreType.DMA((chunks,)),
            pltpu.SemaphoreType.DMA((2,)),
        ],
        compiler_params=pltpu.CompilerParams(
            collective_id=1, has_side_effects=True, vmem_limit_bytes=40 * 2**20
        ),
        name="project",
    )(regrouped, basis)


def on_device(n, groups, demand, initial):
    scale = 1.0 / (demand.shape[0] * demand.shape[2] * groups)
    regrouped, local_gram = exchange_gram(demand, n, groups, scale)
    basis = iterate(sum_gram(local_gram, n, groups), initial)
    core = project(regrouped, basis, n)
    return (basis, jnp.transpose(core, (1, 0, 2)))


def solution(mesh):
    in_specs = (P(None, "gx", "gy"), P())
    out_specs = (P(), P("gx", None, "gy"))
    return jax.shard_map(
        functools.partial(on_device, mesh.shape["gx"], mesh.shape["gy"]),
        mesh=mesh,
        in_specs=in_specs,
        out_specs=out_specs,
        check_vma=False,
    )
```
